32 devices in a mesh: seq: 8 (over y, x, core), tensor: 4 (over z).
Axes of the slice: x: 2, y: 2, z: 4, core: 2. Of those that a mesh axis runs over, the one named last changes fastest.
Arguments:
- tokens: bfloat16 [2048, 8192], P('seq', 'tensor'), may hold values from -24 to 24
- cotangent: bfloat16 [2048, 8192], P('seq', 'tensor'), may hold values from -6 to 6
- w_query: bfloat16 [8192, 4096], P(None, 'tensor'), may hold values from -1 to 1
- w_key: bfloat16 [8192, 1024], P(None, 'tensor'), may hold values from -1 to 1
- w_value: bfloat16 [8192, 1024], P(None, 'tensor'), may hold values from -0.0625 to 0.0625
- w_output: bfloat16 [4096, 8192], P('tensor'), may hold values from -0.09375 to 0.09375
- segments: int32 [2048], replicated, may hold values from 0 to 7, never falling along the last dimension, each value on 1 to 1024 neighbouring positions
- band: int32 [1], replicated, may hold values from 0 to 2047
Outputs:
- layer_out: bfloat16 [2048, 8192], P('seq', 'tensor')
- grad_tokens: bfloat16 [2048, 8192], P('seq', 'tensor')
- grad_query: float32 [8192, 4096], P('seq', 'tensor')
- grad_key: float32 [8192, 1024], P('seq', 'tensor')
- grad_value: float32 [8192, 1024], P('seq', 'tensor')
- grad_output: float32 [4096, 8192], P('tensor', 'seq')
The draws below stay inside these ranges and needn't reach their ends.
All inputs are finite; a program needn't handle non-finite values.
Results may differ from the reference program's by a relative error of at most 0.025.
The reference program's roundings to bfloat16 on the way (of `attend_b`, `heads`, `grad_heads` and `score_grad`) count: a program that leaves them out, or rounds other values in their place, can miss the bound.
Values may be sent and summed in bfloat16 or wider, within the bound.
A program may use at most 320 MiB of HBM per device.

```python
import math
import jax
import jax.numpy as jnp
import numpy as np
from jax import lax

D = 8192
HD = 128
HQ = 32
KVH = 8
TOK_DEV = 256
TOKENS = 2048
N_SEQ = 8
N_TENSOR = 4


def draw_tokens(key, part):
    base = jax.random.normal(jax.random.fold_in(key, 11), (TOKENS, D), jnp.float32)
    values = base
    return jnp.clip(values, -24.0, 24.0).astype(jnp.bfloat16)


def query_weight(key):
    inner = jax.random.fold_in(key, 21)
    weight = jnp.clip(jax.random.normal(inner, (D, HQ * HD), jnp.float32), -4.0, 4.0) / math.sqrt(D)
    return weight


def draw_w_query(key, part):
    return query_weight(key).astype(jnp.bfloat16)


def draw_w_key(key, part):
    own = jnp.clip(jax.random.normal(jax.random.fold_in(key, 22), (D, KVH * HD), jnp.float32), -4.0, 4.0) / math.sqrt(D)
    return own.astype(jnp.bfloat16)


def levels(rng, dims, pieces, low, top_value):
    def one(position, shards_of):
        draws = jax.random.uniform(jax.random.fold_in(jax.random.fold_in(rng, 6), position), (shards_of,), jnp.float32, low / len(pieces), top_value / len(pieces))
        return jnp.repeat(jnp.exp(draws), dims[position] // shards_of).reshape((-1,) + (1,) * (len(dims) - position - 1))

    gain = one(*pieces[0])
    for cut in pieces[1:]:
        gain = gain * one(*cut)
    return gain


def split_up(number_of, total, most, slope):
    portions = [(1 << 20) // math.isqrt(rank ** slope) + 1 for rank in range(2, number_of + 1)]
    rest, given = total - most - (number_of - 1), [1] * (number_of - 1)
    while rest > 0:
        candidates = [i for i in range(number_of - 1) if given[i] < most]
        whole, left = sum([portions[i] for i in candidates]), rest
        for i in candidates:
            more = min(most - given[i], max(1, left * portions[i] // whole), rest)
            given[i] = given[i] + more
            rest = rest - more
    return np.array([most] + given)


def uneven(key, number_of, total, bound, lean):
    if number_of == 2:
        one = jax.random.randint(key, (), max(1, total - bound), min(bound, total - 1) + 1)
        return jnp.stack([one, total - one])
    sizes = jnp.asarray(split_up(number_of, total, bound, lean), jnp.int32)
    pairs = (number_of - 1) // 2
    donor, receiver = sizes[1:1 + 2 * pairs:2], sizes[2:2 + 2 * pairs:2]
    room = jnp.minimum(donor - 1, bound - receiver)
    shifted = jax.random.randint(jax.random.fold_in(key, 1), (pairs,), 0, 1 << 20) % (room + 1)
    sizes = sizes.at[1:1 + 2 * pairs:2].set(donor - shifted).at[2:2 + 2 * pairs:2].set(receiver + shifted)
    return sizes[jax.random.permutation(jax.random.fold_in(key, 2), number_of)]


def bell_draw(stream_key, shape, scale, bound, shards=(), kind=jnp.bfloat16):
    result = jax.random.normal(stream_key, shape, jnp.float32) * scale
    if len(shards) > 0:
        result = levels(stream_key, shape, shards, -0.22, 0.18) * result
    return jnp.clip(result, min=-bound, max=bound).astype(kind)


def setup_inputs(seed: int = 0) -> dict:
    key_of = jax.random.split(jax.random.key(seed), 9)
    tokens = draw_tokens(jax.random.fold_in(key_of[8], 71), 0)
    cotangent = bell_draw(key_of[1], (TOKENS, D), 1.0, 6.0, ((0, 8), (1, 4)))
    w_query = draw_w_query(jax.random.fold_in(key_of[8], 71), 0)
    w_key = draw_w_key(jax.random.fold_in(key_of[8], 71), 0)
    w_value = bell_draw(key_of[4], (D, KVH * HD), D ** -0.5, 0.0625, ((1, 4),))
    w_output = bell_draw(key_of[5], (HQ * HD, D), (HQ * HD) ** -0.5, 0.09375, ((0, 4),))
    segments = jnp.searchsorted(jnp.cumsum(uneven(key_of[6], 8, TOKENS, TOKENS // 2, 2)), jnp.arange(TOKENS), side="right").astype(jnp.int32)
    band = jax.random.randint(key_of[7], (1,), 0, TOKENS).astype(jnp.int32)
    return dict(tokens=tokens, cotangent=cotangent, w_query=w_query, w_key=w_key, w_value=w_value, w_output=w_output, segments=segments, band=band)


def tables(positions, width):
    half = width // 2
    freq = jnp.exp(-math.log(10000.0) * jnp.arange(half, dtype=jnp.float32) * 2.0 / width)
    angles = positions[:, None] * freq[None, :]
    return (jnp.cos(angles), jnp.sin(angles))

def rotate(values, cosine, sine, width):
    shaped = values.reshape(values.shape[0], -1, width)
    half = width // 2
    first = shaped[..., :half]
    second = shaped[..., half:]
    cos_b = cosine[:, None, :]
    sin_b = sine[:, None, :]
    turned = jnp.concatenate([first * cos_b - second * sin_b, second * cos_b + first * sin_b], -1)
    return turned.reshape(values.shape)

def rotate_back(values, cosine, sine, width):
    shaped = values.reshape(values.shape[0], -1, width)
    half = width // 2
    first = shaped[..., :half]
    second = shaped[..., half:]
    cos_b = cosine[:, None, :]
    sin_b = sine[:, None, :]
    turned = jnp.concatenate([first * cos_b + second * sin_b, second * cos_b - first * sin_b], -1)
    return turned.reshape(values.shape)

def reference(tokens, cotangent, w_query, w_key, w_value, w_output, segments, band):
    f32 = jnp.float32
    bf16 = jnp.bfloat16
    factor = 1.0 / math.sqrt(HD)
    group = HQ // KVH
    proj_q = jnp.dot(tokens, w_query, preferred_element_type=f32)
    proj_k = jnp.dot(tokens, w_key, preferred_element_type=f32)
    proj_v = jnp.dot(tokens, w_value, preferred_element_type=f32)
    cosine, sine = tables(jnp.arange(TOKENS).astype(f32), HD)
    query = rotate(proj_q, cosine, sine, HD).astype(bf16)
    keys = rotate(proj_k, cosine, sine, HD).astype(bf16)
    values = proj_v.astype(bf16)
    grad_heads = jnp.dot(cotangent, w_output.T, preferred_element_type=f32).astype(bf16)
    positions = jnp.arange(TOKENS)
    allowed = (segments[:, None] == segments[None, :]) & (positions[None, :] <= positions[:, None] + band[0])
    query_g = query.reshape(TOKENS, KVH, group, HD).transpose(1, 0, 2, 3)
    grad_g = grad_heads.reshape(TOKENS, KVH, group, HD).transpose(1, 0, 2, 3)
    keys_g = keys.reshape(TOKENS, KVH, HD).transpose(1, 0, 2)
    values_g = values.reshape(TOKENS, KVH, HD).transpose(1, 0, 2)

    def one_group(item):
        q_part, k_part, v_part, g_part = item
        q32 = q_part.astype(f32)
        k32 = k_part.astype(f32)
        v32 = v_part.astype(f32)
        g32 = g_part.astype(f32)
        scores = jnp.einsum('ird,jd->rij', q32, k32) * factor
        masked = jnp.where(allowed[None], scores, -1e+30)
        top = lax.optimization_barrier(jnp.max(masked, -1, keepdims=True))
        expo = jnp.exp(masked - top)
        attend = expo / lax.optimization_barrier(jnp.sum(expo, -1, keepdims=True))
        attend_b = attend.astype(bf16)
        heads = jnp.einsum('rij,jd->ird', attend_b.astype(f32), v32).astype(bf16)
        delta = lax.optimization_barrier(jnp.sum(g32 * heads.astype(f32), -1)).T
        dprob = jnp.einsum('ird,jd->rij', g32, v32)
        score_grad = (attend * (dprob - delta[:, :, None])).astype(bf16).astype(f32)
        query_grad = jnp.einsum('rij,jd->ird', score_grad, k32) * factor
        key_grad = jnp.einsum('rij,ird->jd', score_grad, q32) * factor
        value_grad = jnp.einsum('rij,ird->jd', attend_b.astype(f32), g32)
        return (heads, query_grad, key_grad, value_grad)
    heads, query_grad, key_grad, value_grad = lax.map(one_group, (query_g, keys_g, values_g, grad_g))
    heads = heads.transpose(1, 0, 2, 3).reshape(TOKENS, HQ * HD)
    query_grad = query_grad.transpose(1, 0, 2, 3).reshape(TOKENS, HQ * HD)
    key_grad = key_grad.transpose(1, 0, 2).reshape(TOKENS, KVH * HD)
    value_grad = value_grad.transpose(1, 0, 2).reshape(TOKENS, KVH * HD)
    pre_q = rotate_back(query_grad, cosine, sine, HD).astype(bf16)
    pre_k = rotate_back(key_grad, cosine, sine, HD).astype(bf16)
    pre_v = value_grad.astype(bf16)
    q_width = HQ // N_TENSOR * HD
    k_width = KVH // N_TENSOR * HD
    heads_t = heads.reshape(TOKENS, N_TENSOR, q_width).transpose(1, 0, 2)
    out_t = w_output.reshape(N_TENSOR, q_width, D)
    pre_q_t = pre_q.reshape(TOKENS, N_TENSOR, q_width).transpose(1, 0, 2)
    pre_k_t = pre_k.reshape(TOKENS, N_TENSOR, k_width).transpose(1, 0, 2)
    pre_v_t = pre_v.reshape(TOKENS, N_TENSOR, k_width).transpose(1, 0, 2)
    wq_t = w_query.reshape(D, N_TENSOR, q_width).transpose(1, 0, 2)
    wk_t = w_key.reshape(D, N_TENSOR, k_width).transpose(1, 0, 2)
    wv_t = w_value.reshape(D, N_TENSOR, k_width).transpose(1, 0, 2)

    def add_group(carry, item):
        out_sum, grad_sum = carry
        h_part, o_part, pq, pk, pv, wq, wk, wv = item
        first = jnp.dot(h_part, o_part, preferred_element_type=f32).astype(bf16)
        second = (jnp.dot(pq, wq.T, preferred_element_type=f32) + jnp.dot(pk, wk.T, preferred_element_type=f32) + jnp.dot(pv, wv.T, preferred_element_type=f32)).astype(bf16)
        first, second = lax.optimization_barrier((first, second))
        return ((out_sum + first.astype(f32), grad_sum + second.astype(f32)), None)
    zeros_td = jnp.zeros((TOKENS, D), f32)
    (layer_out, grad_tokens), _ = lax.scan(add_group, (zeros_td, zeros_td), (heads_t, out_t, pre_q_t, pre_k_t, pre_v_t, wq_t, wk_t, wv_t))
    rows_cat = jnp.concatenate([pre_q, pre_k, pre_v], 1)
    shard_x = tokens.reshape(N_SEQ, TOK_DEV, D)
    shard_d = rows_cat.reshape(N_SEQ, TOK_DEV, -1)
    shard_h = heads.reshape(N_SEQ, TOK_DEV, HQ * HD)
    shard_g = cotangent.reshape(N_SEQ, TOK_DEV, D)

    def add_shard(carry, item):
        left_sum, right_sum = carry
        part_x, part_d, part_h, part_g = item
        left = jnp.dot(part_x.T, part_d, preferred_element_type=f32).astype(bf16)
        right = jnp.dot(part_h.T, part_g, preferred_element_type=f32).astype(bf16)
        left, right = lax.optimization_barrier((left, right))
        return ((left_sum + left.astype(f32), right_sum + right.astype(f32)), None)
    start_carry = (jnp.zeros((D, rows_cat.shape[1]), f32), jnp.zeros((HQ * HD, D), f32))
    (left_sum, grad_output), _ = lax.scan(add_shard, start_carry, (shard_x, shard_d, shard_h, shard_g))
    grad_query = left_sum[:, :HQ * HD]
    grad_key = left_sum[:, HQ * HD:HQ * HD + KVH * HD]
    grad_value = left_sum[:, HQ * HD + KVH * HD:]
    return (layer_out.astype(bf16), grad_tokens.astype(bf16), grad_query, grad_key, grad_value, grad_output)
```

```python
import math

import jax
import jax.numpy as jnp
from jax import lax
from jax.sharding import PartitionSpec as P

HD = 128


def tables(positions, width):
    half = width // 2
    freq = jnp.exp(-math.log(10000.0) * jnp.arange(half, dtype=jnp.float32) * 2.0 / width)
    angles = positions[:, None] * freq[None, :]
    return (jnp.cos(angles), jnp.sin(angles))


def rotate(values, cosine, sine, width):
    shaped = values.reshape(values.shape[0], -1, width)
    half = width // 2
    first = shaped[..., :half]
    second = shaped[..., half:]
    cos_b = cosine[:, None, :]
    sin_b = sine[:, None, :]
    turned = jnp.concatenate([first * cos_b - second * sin_b, second * cos_b + first * sin_b], -1)
    return turned.reshape(values.shape)


def rotate_back(values, cosine, sine, width):
    shaped = values.reshape(values.shape[0], -1, width)
    half = width // 2
    first = shaped[..., :half]
    second = shaped[..., half:]
    cos_b = cosine[:, None, :]
    sin_b = sine[:, None, :]
    turned = jnp.concatenate([first * cos_b + second * sin_b, second * cos_b - first * sin_b], -1)
    return turned.reshape(values.shape)


def contract_last(left, right):
    return lax.dot_general(
        left, right, (((1,), (1,)), ((), ())), preferred_element_type=jnp.float32
    )


def contract_first(left, right):
    return lax.dot_general(
        left, right, (((0,), (0,)), ((), ())), preferred_element_type=jnp.float32
    )


def swap(value, step):
    count = lax.axis_size("seq")
    return lax.ppermute(value, "seq", [(i, i ^ step) for i in range(count)])


def block_order(count):
    return list(range(0, count, 2)) + list(range(1, count, 2))


def gather_blocks(value):
    count = lax.axis_size("seq")
    even = [value] + [swap(value, step) for step in range(2, count, 2)]
    odd = [swap(piece, 1) for piece in even]
    return even + odd


def scatter_sum(pieces):
    f32 = jnp.float32
    half = len(pieces) // 2
    given = [swap(piece.astype(jnp.bfloat16), 1) for piece in pieces[half:]]
    paired = [pieces[k].astype(f32) + given[k].astype(f32) for k in range(half)]
    total = paired[0]
    for k in range(1, half):
        total = total + swap(paired[k].astype(jnp.bfloat16), 2 * k).astype(f32)
    return total


def reshard_columns(full):
    return lax.all_to_all(full, "seq", 1, 0, tiled=True)


def in_order(pieces, me):
    count = len(pieces)
    rows, columns = pieces[0].shape
    whole = jnp.zeros((count * rows, columns), pieces[0].dtype)
    for piece, step in zip(pieces, block_order(count)):
        whole = lax.dynamic_update_slice(whole, piece, ((me ^ step) * rows, 0))
    return whole


def after(value, *earlier):
    return lax.optimization_barrier((value, *earlier))[0]


def on_device(tokens, cotangent, w_query, w_key, w_value, w_output, segments, band):
    f32 = jnp.float32
    bf16 = jnp.bfloat16
    factor = 1.0 / math.sqrt(HD)
    tok_rows = tokens.shape[0]
    seq_count = lax.axis_size("seq")
    all_rows = tok_rows * seq_count
    q_width = w_query.shape[1]
    k_width = w_key.shape[1]
    kv_local = k_width // HD
    group = q_width // k_width
    me = lax.axis_index("seq")
    order = block_order(seq_count)

    full_x = lax.all_gather(tokens, "tensor", axis=1, tiled=True)
    full_grad = lax.all_gather(after(cotangent, full_x), "tensor", axis=1, tiled=True)

    first_row = me * tok_rows
    own_rows = first_row + jnp.arange(tok_rows)
    cosine, sine = tables(own_rows.astype(f32), HD)
    proj_k = jnp.dot(full_x, w_key, preferred_element_type=f32)
    proj_v = jnp.dot(full_x, w_value, preferred_element_type=f32)
    keys_local = rotate(proj_k, cosine, sine, HD).astype(bf16)
    values_local = proj_v.astype(bf16)
    kv_pieces = gather_blocks(jnp.concatenate([keys_local, values_local], 1))
    kv_all = jnp.concatenate(kv_pieces, 0)
    keys, values = kv_all[:, :k_width], kv_all[:, k_width:]
    proj_q = jnp.dot(full_x, w_query, preferred_element_type=f32)
    query = rotate(proj_q, cosine, sine, HD).astype(bf16)

    x_cols = reshard_columns(full_x)

    key_rows = jnp.concatenate([(me ^ step) * tok_rows + jnp.arange(tok_rows) for step in order])
    key_seg = jnp.concatenate(
        [lax.dynamic_slice_in_dim(segments, (me ^ step) * tok_rows, tok_rows) for step in order]
    )
    own_seg = lax.dynamic_slice_in_dim(segments, first_row, tok_rows)
    allowed = (own_seg[:, None] == key_seg[None, :]) & (
        key_rows[None, :] <= own_rows[:, None] + band[0]
    )
    query4 = query.reshape(tok_rows, kv_local, group, HD)
    keys3 = keys.reshape(all_rows, kv_local, HD)
    values3 = values.reshape(all_rows, kv_local, HD)
    scores = jnp.einsum("igrd,jgd->grij", query4, keys3, preferred_element_type=f32) * factor
    masked = jnp.where(allowed[None, None], scores, -1e30)
    top = jnp.max(masked, -1, keepdims=True)
    expo = jnp.exp(masked - top)
    attend = expo / jnp.sum(expo, -1, keepdims=True)
    attend_b = attend.astype(bf16)
    heads4 = jnp.einsum("grij,jgd->igrd", attend_b, values3, preferred_element_type=f32).astype(
        bf16
    )
    heads = heads4.reshape(tok_rows, -1)
    out_part = jnp.dot(heads, w_output, preferred_element_type=f32).astype(bf16)
    layer_out = lax.psum_scatter(out_part, "tensor", scatter_dimension=1, tiled=True)

    full_grad = after(full_grad, out_part)
    g_cols = reshard_columns(full_grad)
    heads_all = in_order(gather_blocks(heads), me)
    grad_heads = after(contract_last(full_grad, w_output).astype(bf16), x_cols)
    grad4 = grad_heads.reshape(tok_rows, kv_local, group, HD)
    delta = jnp.sum(grad4.astype(f32) * heads4.astype(f32), -1).transpose(1, 2, 0)
    dprob = jnp.einsum("igrd,jgd->grij", grad4, values3, preferred_element_type=f32)
    score_grad = (attend * (dprob - delta[..., None])).astype(bf16)
    query_grad = (
        jnp.einsum("grij,jgd->igrd", score_grad, keys3, preferred_element_type=f32) * factor
    )
    key_part = jnp.einsum("grij,igrd->jgd", score_grad, query4, preferred_element_type=f32) * factor
    value_part = jnp.einsum("grij,igrd->jgd", attend_b, grad4, preferred_element_type=f32)
    kv_part = jnp.concatenate(
        [key_part.reshape(all_rows, -1), value_part.reshape(all_rows, -1)], 1
    ).astype(bf16)
    kv_part = after(kv_part, g_cols)
    kv_grad = scatter_sum([kv_part[k * tok_rows : (k + 1) * tok_rows] for k in range(seq_count)])
    pre_q = rotate_back(query_grad.reshape(tok_rows, -1), cosine, sine, HD).astype(bf16)
    pre_k = rotate_back(kv_grad[:, :k_width], cosine, sine, HD).astype(bf16)
    pre_v = kv_grad[:, k_width:].astype(bf16)
    grad_part = (
        contract_last(pre_q, w_query) + contract_last(pre_k, w_key) + contract_last(pre_v, w_value)
    ).astype(bf16)
    grad_tokens = lax.psum_scatter(grad_part, "tensor", scatter_dimension=1, tiled=True)

    pre_cat = after(jnp.concatenate([pre_q, pre_k, pre_v], 1), heads_all)
    pre_all = in_order(gather_blocks(pre_cat), me)
    grad_output = contract_first(heads_all, g_cols)
    merged = contract_first(x_cols, pre_all)
    grad_query = merged[:, :q_width]
    grad_key = merged[:, q_width : q_width + k_width]
    grad_value = merged[:, q_width + k_width :]
    return (layer_out, grad_tokens, grad_query, grad_key, grad_value, grad_output)


def solution(mesh):
    in_specs = (
        P("seq", "tensor"),
        P("seq", "tensor"),
        P(None, "tensor"),
        P(None, "tensor"),
        P(None, "tensor"),
        P("tensor", None),
        P(),
        P(),
    )
    out_specs = (
        P("seq", "tensor"),
        P("seq", "tensor"),
        P("seq", "tensor"),
        P("seq", "tensor"),
        P("seq", "tensor"),
        P("tensor", "seq"),
    )
    return jax.shard_map(
        on_device, mesh=mesh, in_specs=in_specs, out_specs=out_specs, check_vma=False
    )
```

```python
import math

import jax
import jax.numpy as jnp
from jax import lax
from jax.sharding import PartitionSpec as P

HD = 128


def tables(positions, width):
    half = width // 2
    freq = jnp.exp(-math.log(10000.0) * jnp.arange(half, dtype=jnp.float32) * 2.0 / width)
    angles = positions[:, None] * freq[None, :]
    return (jnp.cos(angles), jnp.sin(angles))


def rotate(values, cosine, sine, width):
    shaped = values.reshape(values.shape[0], -1, width)
    half = width // 2
    first = shaped[..., :half]
    second = shaped[..., half:]
    cos_b = cosine[:, None, :]
    sin_b = sine[:, None, :]
    turned = jnp.concatenate([first * cos_b - second * sin_b, second * cos_b + first * sin_b], -1)
    return turned.reshape(values.shape)


def rotate_back(values, cosine, sine, width):
    shaped = values.reshape(values.shape[0], -1, width)
    half = width // 2
    first = shaped[..., :half]
    second = shaped[..., half:]
    cos_b = cosine[:, None, :]
    sin_b = sine[:, None, :]
    turned = jnp.concatenate([first * cos_b + second * sin_b, second * cos_b - first * sin_b], -1)
    return turned.reshape(values.shape)


def contract_last(left, right):
    return lax.dot_general(
        left, right, (((1,), (1,)), ((), ())), preferred_element_type=jnp.float32
    )


def contract_first(left, right):
    return lax.dot_general(
        left, right, (((0,), (0,)), ((), ())), preferred_element_type=jnp.float32
    )


def swap(value, step):
    count = lax.axis_size("seq")
    return lax.ppermute(value, "seq", [(i, i ^ step) for i in range(count)])


def block_order(count):
    return list(range(0, count, 2)) + list(range(1, count, 2))


def gather_blocks(value):
    count = lax.axis_size("seq")
    even = [value] + [swap(value, step) for step in range(2, count, 2)]
    odd = [swap(piece, 1) for piece in even]
    return even + odd


def scatter_sum(pieces):
    f32 = jnp.float32
    half = len(pieces) // 2
    given = [swap(piece.astype(jnp.bfloat16), 1) for piece in pieces[half:]]
    paired = [pieces[k].astype(f32) + given[k].astype(f32) for k in range(half)]
    total = paired[0]
    for k in range(1, half):
        total = total + swap(paired[k].astype(jnp.bfloat16), 2 * k).astype(f32)
    return total


def reshard_columns(full):
    return lax.all_to_all(full, "seq", 1, 0, tiled=True)


def in_order(pieces, me):
    count = len(pieces)
    rows, columns = pieces[0].shape
    whole = jnp.zeros((count * rows, columns), pieces[0].dtype)
    for piece, step in zip(pieces, block_order(count)):
        whole = lax.dynamic_update_slice(whole, piece, ((me ^ step) * rows, 0))
    return whole


def after(value, *earlier):
    return lax.optimization_barrier((value, *earlier))[0]


def on_device(tokens, cotangent, w_query, w_key, w_value, w_output, segments, band):
    f32 = jnp.float32
    bf16 = jnp.bfloat16
    factor = 1.0 / math.sqrt(HD)
    tok_rows = tokens.shape[0]
    seq_count = lax.axis_size("seq")
    all_rows = tok_rows * seq_count
    q_width = w_query.shape[1]
    k_width = w_key.shape[1]
    kv_local = k_width // HD
    group = q_width // k_width
    me = lax.axis_index("seq")
    order = block_order(seq_count)

    full_x = lax.all_gather(tokens, "tensor", axis=1, tiled=True)
    full_grad = lax.all_gather(after(cotangent, full_x), "tensor", axis=1, tiled=True)

    first_row = me * tok_rows
    own_rows = first_row + jnp.arange(tok_rows)
    cosine, sine = tables(own_rows.astype(f32), HD)
    proj_k = jnp.dot(full_x, w_key, preferred_element_type=f32)
    proj_v = jnp.dot(full_x, w_value, preferred_element_type=f32)
    keys_local = rotate(proj_k, cosine, sine, HD).astype(bf16)
    values_local = proj_v.astype(bf16)
    kv_pieces = gather_blocks(jnp.concatenate([keys_local, values_local], 1))
    kv_all = jnp.concatenate(kv_pieces, 0)
    keys, values = kv_all[:, :k_width], kv_all[:, k_width:]
    proj_q = jnp.dot(full_x, w_query, preferred_element_type=f32)
    query = rotate(proj_q, cosine, sine, HD).astype(bf16)

    x_cols = reshard_columns(full_x)

    key_rows = jnp.concatenate([(me ^ step) * tok_rows + jnp.arange(tok_rows) for step in order])
    key_seg = jnp.concatenate(
        [lax.dynamic_slice_in_dim(segments, (me ^ step) * tok_rows, tok_rows) for step in order]
    )
    own_seg = lax.dynamic_slice_in_dim(segments, first_row, tok_rows)
    allowed = (own_seg[:, None] == key_seg[None, :]) & (
        key_rows[None, :] <= own_rows[:, None] + band[0]
    )
    query4 = query.reshape(tok_rows, kv_local, group, HD)
    keys3 = keys.reshape(all_rows, kv_local, HD)
    values3 = values.reshape(all_rows, kv_local, HD)
    scores = jnp.einsum("igrd,jgd->grij", query4, keys3, preferred_element_type=f32) * factor
    masked = jnp.where(allowed[None, None], scores, -1e30)
    top = jnp.max(masked, -1, keepdims=True)
    expo = jnp.exp(masked - top)
    attend = expo / jnp.sum(expo, -1, keepdims=True)
    attend_b = attend.astype(bf16)
    heads4 = jnp.einsum("grij,jgd->igrd", attend_b, values3, preferred_element_type=f32).astype(
        bf16
    )
    heads = heads4.reshape(tok_rows, -1)
    out_part = jnp.dot(heads, w_output, preferred_element_type=f32).astype(bf16)
    out_part, full_grad = lax.optimization_barrier((out_part, full_grad))
    layer_out = lax.psum_scatter(out_part, "tensor", scatter_dimension=1, tiled=True)

    g_cols = reshard_columns(full_grad)
    heads_all = in_order(gather_blocks(heads), me)
    grad_heads = after(contract_last(full_grad, w_output).astype(bf16), x_cols)
    grad4 = grad_heads.reshape(tok_rows, kv_local, group, HD)
    delta = jnp.sum(grad4.astype(f32) * heads4.astype(f32), -1).transpose(1, 2, 0)
    dprob = jnp.einsum("igrd,jgd->grij", grad4, values3, preferred_element_type=f32)
    score_grad = (attend * (dprob - delta[..., None])).astype(bf16)
    query_grad = (
        jnp.einsum("grij,jgd->igrd", score_grad, keys3, preferred_element_type=f32) * factor
    )
    key_part = jnp.einsum("grij,igrd->jgd", score_grad, query4, preferred_element_type=f32) * factor
    value_part = jnp.einsum("grij,igrd->jgd", attend_b, grad4, preferred_element_type=f32)
    kv_part = jnp.concatenate(
        [key_part.reshape(all_rows, -1), value_part.reshape(all_rows, -1)], 1
    ).astype(bf16)
    kv_grad = scatter_sum([kv_part[k * tok_rows : (k + 1) * tok_rows] for k in range(seq_count)])
    kv_grad = after(kv_grad, g_cols)
    pre_q = rotate_back(query_grad.reshape(tok_rows, -1), cosine, sine, HD).astype(bf16)
    pre_k = rotate_back(kv_grad[:, :k_width], cosine, sine, HD).astype(bf16)
    pre_v = kv_grad[:, k_width:].astype(bf16)
    grad_part = (
        contract_last(pre_q, w_query) + contract_last(pre_k, w_key) + contract_last(pre_v, w_value)
    ).astype(bf16)
    grad_tokens = lax.psum_scatter(grad_part, "tensor", scatter_dimension=1, tiled=True)

    pre_cat = after(jnp.concatenate([pre_q, pre_k, pre_v], 1), heads_all)
    pre_all = in_order(gather_blocks(pre_cat), me)
    grad_output = contract_first(heads_all, g_cols)
    merged = contract_first(x_cols, pre_all)
    grad_query = merged[:, :q_width]
    grad_key = merged[:, q_width : q_width + k_width]
    grad_value = merged[:, q_width + k_width :]
    return (layer_out, grad_tokens, grad_query, grad_key, grad_value, grad_output)


def solution(mesh):
    in_specs = (
        P("seq", "tensor"),
        P("seq", "tensor"),
        P(None, "tensor"),
        P(None, "tensor"),
        P(None, "tensor"),
        P("tensor", None),
        P(),
        P(),
    )
    out_specs = (
        P("seq", "tensor"),
        P("seq", "tensor"),
        P("seq", "tensor"),
        P("seq", "tensor"),
        P("seq", "tensor"),
        P("tensor", "seq"),
    )
    return jax.shard_map(
        on_device, mesh=mesh, in_specs=in_specs, out_specs=out_specs, check_vma=False
    )
```
